32 devices in a mesh: row: 8 (over y, x, core), col: 4 (over z).
Axes of the slice: x: 2, y: 2, z: 4, core: 2. Of those that a mesh axis runs over, the one named last changes fastest.
Arguments:
- tokens: bfloat16 [384, 8192], P('col', 'row'), may hold values from -6 to 6
- gate_weight: bfloat16 [8192, 29568], P('row', 'col'), may hold values from -0.0625 to 0.0625
- up_weight: bfloat16 [8192, 29568], P('row', 'col'), may hold values from -0.0625 to 0.0625
- gate_lower: bfloat16 [16, 8192, 64], P('col', 'row'), may hold values from -0.0625 to 0.0625
- up_lower: bfloat16 [16, 8192, 64], P('col', 'row'), may hold values from -0.0625 to 0.0625
- gate_upper: bfloat16 [16, 64, 29568], P('row', None, 'col'), may hold values from -0.21875 to 0.21875
- up_upper: bfloat16 [16, 64, 29568], P('row', None, 'col'), may hold values from -0.21875 to 0.21875
- outgoing: int32 [1], replicated, may hold values from 0 to 15
- incoming: int32 [1], replicated, may hold values from 0 to 15
Outputs:
- new_gate: bfloat16 [8192, 29568], P('row', 'col')
- new_up: bfloat16 [8192, 29568], P('row', 'col')
- hidden: bfloat16 [384, 29568], P('row', 'col')
The draws below stay inside these ranges and needn't reach their ends.
All inputs are finite; a program needn't handle non-finite values.
Results may differ from the reference program's by a relative error of at most 0.0058.
Values may be sent and summed in bfloat16 or wider, within the bound.
No kernel may reach another device: no remote copies, remote signals or barrier semaphores. Data moves between devices by JAX's collectives and lax.ppermute only.
A program may use at most 192 MiB of HBM per device.

```python
import jax
import jax.numpy as jnp
from jax import lax

D = 8192
FF = 29568
R = 64
TENANTS = 16
TOKENS = 384
N_ROW = 8


def levels(rng, dims, cuts, smallest, largest):
    level = 1.0
    for dim, blocks in cuts:
        draws = jax.random.uniform(jax.random.fold_in(jax.random.fold_in(rng, 6), dim), (blocks,), jnp.float32, smallest / len(cuts), largest / len(cuts))
        level = level * jnp.repeat(jnp.exp(draws), dims[dim] // blocks).reshape((-1,) + (1,) * (len(dims) - 1 - dim))
    return level


def normal_values(own_key, extent, deviation, limit, pieces=(), held_as=jnp.bfloat16):
    values = deviation * jax.random.normal(own_key, extent, jnp.float32)
    if pieces:
        values = values * levels(own_key, extent, pieces, -0.22, 0.18)
    return jnp.clip(values, -limit, limit).astype(held_as)


def setup_inputs(seed: int = 0) -> dict:
    arg_keys = jax.random.split(jax.random.key(seed), 10)
    tokens = normal_values(arg_keys[0], (TOKENS, D), 1.0, 6.0, ((0, 4), (1, 8)))
    gate_weight = normal_values(arg_keys[1], (D, FF), D ** -0.5, 0.0625, ((0, 8), (1, 4)))
    up_weight = normal_values(arg_keys[2], (D, FF), D ** -0.5, 0.0625, ((0, 8), (1, 4)))
    gate_lower = normal_values(arg_keys[3], (TENANTS, D, R), D ** -0.5, 0.0625, ((0, 4), (1, 8)))
    up_lower = normal_values(arg_keys[4], (TENANTS, D, R), D ** -0.5, 0.0625, ((0, 4), (1, 8)))
    gate_upper = normal_values(arg_keys[5], (TENANTS, R, FF), (12 * R) ** -0.5, 0.21875, ((0, 8), (2, 4)))
    up_upper = normal_values(arg_keys[6], (TENANTS, R, FF), (12 * R) ** -0.5, 0.21875, ((0, 8), (2, 4)))
    outgoing = jax.random.randint(arg_keys[7], (1,), 0, TENANTS).astype(jnp.int32)
    incoming = jax.random.randint(arg_keys[8], (1,), 0, TENANTS).astype(jnp.int32)
    return dict(tokens=tokens, gate_weight=gate_weight, up_weight=up_weight, gate_lower=gate_lower, up_lower=up_lower, gate_upper=gate_upper, up_upper=up_upper, outgoing=outgoing, incoming=incoming)


def merge_one(weight, lower, upper, old, new):
    lower_old = lax.dynamic_index_in_dim(lower, old, 0, keepdims=False)
    lower_new = lax.dynamic_index_in_dim(lower, new, 0, keepdims=False)
    upper_old = lax.dynamic_index_in_dim(upper, old, 0, keepdims=False)
    upper_new = lax.dynamic_index_in_dim(upper, new, 0, keepdims=False)
    blocks = N_ROW
    weight_blocks = weight.reshape(blocks, D // blocks, FF)
    lower_old = lower_old.reshape(blocks, D // blocks, R)
    lower_new = lower_new.reshape(blocks, D // blocks, R)

    def one_block(items):
        w_block, l_old, l_new = items
        delta = jnp.dot(l_new, upper_new, preferred_element_type=jnp.float32) - jnp.dot(l_old, upper_old, preferred_element_type=jnp.float32)
        return (w_block.astype(jnp.float32) + delta).astype(jnp.bfloat16)

    merged = lax.map(one_block, (weight_blocks, lower_old, lower_new))
    return merged.reshape(D, FF)


def reference(tokens, gate_weight, up_weight, gate_lower, up_lower, gate_upper, up_upper, outgoing, incoming):
    old = outgoing[0].astype(jnp.int32)
    new = incoming[0].astype(jnp.int32)
    new_gate = merge_one(gate_weight, gate_lower, gate_upper, old, new)
    new_up = merge_one(up_weight, up_lower, up_upper, old, new)
    gate = jnp.dot(tokens, new_gate, preferred_element_type=jnp.float32)
    up = jnp.dot(tokens, new_up, preferred_element_type=jnp.float32)
    hidden = (jax.nn.silu(gate) * up).astype(jnp.bfloat16)
    return new_gate, new_up, hidden
```

```python
import functools

import jax
import jax.numpy as jnp
from jax import lax
from jax.experimental import pallas as pl
from jax.experimental.pallas import tpu as pltpu
from jax.sharding import PartitionSpec as P

TILE = 512
SUB = 256
CHUNKS = 3
F32 = jnp.float32
BF16 = jnp.bfloat16
SMALL = pl.CostEstimate(flops=1024, bytes_accessed=1024, transcendentals=0)
COST = pl.CostEstimate(flops=2**34, bytes_accessed=2**25, transcendentals=0)
VMEM = pl.BlockSpec(memory_space=pltpu.VMEM)


def after(value, others):
    return lax.optimization_barrier((value, others))[0]


def bit(value, which):
    return (value >> which) & 1


def swap(value, axis, size, distance):
    return lax.ppermute(value, axis, [(i, i ^ distance) for i in range(size)])


def block_order(bits):
    offsets = range(0, 2 ** (len(bits) + 1), 2)
    return sorted(offsets, key=lambda k: tuple(-bit(k, b) for b in bits))


class Factor:
    def __init__(self, axis, size, index, bits, held, sent, owner):
        self.axis, self.size, self.index, self.bits = axis, size, index, bits
        self.held, self.owner = held, owner
        self.arrived = [swap(sent, axis, size, 1 << bits[0])]
        self.last = bits[0]
        self.todo = [("scatter", b) for b in bits[1:]] + [("turn", bits[-1])]
        self.todo += [("gather", b) for b in reversed(bits[:-1])]

    def chosen(self):
        mine = bit(self.index, self.last)
        return jnp.where(mine == bit(self.owner, self.last), self.held, self.arrived[0])

    def joined(self):
        low = jnp.concatenate([self.held, self.arrived[0]], axis=0)
        high = jnp.concatenate([self.arrived[0], self.held], axis=0)
        return jnp.where(bit(self.index, self.last) == 0, low, high)

    def step(self):
        kind, b = self.todo.pop(0)
        if kind == "scatter":
            value = self.chosen()
            half = value.shape[0] // 2
            mine = bit(self.index, b)
            sent = lax.dynamic_slice_in_dim(value, (1 - mine) * half, half, 0)
            self.held = lax.dynamic_slice_in_dim(value, mine * half, half, 0)
        else:
            self.held = sent = self.chosen() if kind == "turn" else self.joined()
        self.arrived = [swap(sent, self.axis, self.size, 1 << b)]
        self.last = b
        return sent


def tokens_kernel(rows, at, *refs):
    first = 0
    for ref in refs[:-1]:
        for h in range(ref.shape[0] // rows):
            start = pl.multiple_of(at[first + h] * rows, rows)
            refs[-1][pl.ds(start, rows), :] = ref[h * rows : (h + 1) * rows, :]
        first += ref.shape[0] // rows


def ordered_tokens(parts, offsets, n_row, row, col, bits):
    rows = sum(part.shape[0] for part in parts) // n_row
    blocks = n_row // len(offsets)
    source = (col ^ jnp.array(offsets, jnp.int32))[:, None]
    offset = ((source * blocks + jnp.arange(blocks, dtype=jnp.int32)) ^ row).reshape(-1)
    place = offset * 0
    for b in [0] + bits:
        place = place * 2 + 1 - bit(offset, b)
    return pl.pallas_call(
        functools.partial(tokens_kernel, rows),
        out_shape=jax.ShapeDtypeStruct((rows * n_row, parts[0].shape[1]), BF16),
        in_specs=[pl.BlockSpec(memory_space=pltpu.SMEM)] + [VMEM] * len(parts),
        out_specs=VMEM,
        compiler_params=pltpu.CompilerParams(vmem_limit_bytes=12 * 2**20),
        name="order_tokens",
    )(place, *parts)


def times_transposed(left, right):
    return lax.dot_general(left, right, (((1,), (1,)), ((), ())), preferred_element_type=F32)


def multiply_kernel(rows, places, tok, gate_w, up_w, away, gate_home, up_home):
    half = tok.shape[0] // 2
    part = times_transposed(tok[...], gate_w[...])
    away[:half, :] = part[:half].astype(BF16)
    gate_home[...] = part[half:]
    part = times_transposed(tok[...], up_w[...])
    for to, at in enumerate(places):
        into = slice(to * rows, (to + 1) * rows)
        away[half + to * rows : half + (to + 1) * rows, :] = part[at * rows :][:rows].astype(BF16)
        up_home[into, :] = part[half + at * rows :][:rows]


def multiply_chunk(span, columns, weights, tok, rows, places):
    first, count = span
    n_tok, depth = tok.shape
    half = n_tok // 2
    weight = pl.BlockSpec((TILE, depth), lambda i: (first + i, 0))
    return pl.pallas_call(
        functools.partial(multiply_kernel, rows, places),
        grid=(count,),
        out_shape=[
            jax.ShapeDtypeStruct((n_tok, columns), BF16),
            jax.ShapeDtypeStruct((half, columns), F32),
            jax.ShapeDtypeStruct((half, columns), F32),
        ],
        in_specs=[pl.BlockSpec(tok.shape, lambda i: (0, 0)), weight, weight],
        out_specs=[
            pl.BlockSpec((n_tok, TILE), lambda i: (0, i)),
            pl.BlockSpec((half, TILE), lambda i: (0, i)),
            pl.BlockSpec((half, TILE), lambda i: (0, i)),
        ],
        compiler_params=pltpu.CompilerParams(
            dimension_semantics=("arbitrary",), vmem_limit_bytes=40 * 2**20
        ),
        cost_estimate=COST,
        name="multiply",
    )(tok, *weights)


def lower_kernel(rows, places, tok, low, old_away, old_gate, old_up, away, gate_home, up_home):
    rank = low.shape[0] // 2
    multiply_kernel(
        rows, places, tok, low.at[:rank, :], low.at[rank:, :], away, gate_home, up_home
    )


def multiply_lower(tok, low, part, rows, places):
    rank = low.shape[0] // 2
    last = part[0].shape[1] // rank - 1
    specs = [pl.BlockSpec((array.shape[0], rank), lambda i: (0, last)) for array in part]
    return pl.pallas_call(
        functools.partial(lower_kernel, rows, places),
        grid=(1,),
        out_shape=[jax.ShapeDtypeStruct(array.shape, array.dtype) for array in part],
        in_specs=[pl.BlockSpec(array.shape, lambda i: (0, 0)) for array in (tok, low)] + specs,
        out_specs=specs,
        input_output_aliases={2: 0, 3: 1, 4: 2},
        compiler_params=pltpu.CompilerParams(vmem_limit_bytes=12 * 2**20),
        cost_estimate=SMALL,
        name="multiply_lower",
    )(tok, low, *part)


def merge_kernel(low, gate_w, up_w, gate_b, gate_c, up_b, up_c, *refs):
    rank = gate_b.shape[0]
    for start in range(0, TILE, SUB):
        units = slice(start, start + SUB)
        for t, (weight, mine, other) in enumerate(
            ((gate_w, gate_b, gate_c), (up_w, up_b, up_c))
        ):
            delta = lax.dot_general(
                jnp.concatenate([mine[:, units], other[:, units]], axis=0),
                low[2 * t * rank : 2 * (t + 1) * rank, :],
                (((0,), (0,)), ((), ())),
                preferred_element_type=F32,
            )
            refs[t - 2][units, :] = (weight[units, :].astype(F32) + delta).astype(BF16)


def merge_span(span, weights, low, uppers, merged):
    first, count = span
    units, depth = weights[0].shape
    weight = pl.BlockSpec((TILE, depth), lambda i: (first + i, 0))
    upper = pl.BlockSpec((uppers[0].shape[0], TILE), lambda i: (0, first + i))
    operands = [low, *weights, *uppers, *merged]
    specs = [pl.BlockSpec(low.shape, lambda i: (0, 0)), weight, weight] + [upper] * 4
    specs += [pl.BlockSpec(memory_space=pl.ANY)] * len(merged)
    return pl.pallas_call(
        merge_kernel,
        grid=(count,),
        out_shape=[jax.ShapeDtypeStruct((units, depth), BF16)] * 2,
        in_specs=specs,
        out_specs=[weight] * 2,
        input_output_aliases={7: 0, 8: 1} if merged else {},
        compiler_params=pltpu.CompilerParams(
            dimension_semantics=("arbitrary",), vmem_limit_bytes=40 * 2**20
        ),
        cost_estimate=SMALL,
        name="merge",
    )(*operands)


class Sum:
    def __init__(self, away, gate, up, n_row):
        half = gate.shape[0]
        self.home = [gate, up]
        self.arrived = [swap(away, "row", n_row, 1)]
        self.places = [(0, 0, half), (0, half, half)]
        self.step = 0

    def came(self, t):
        array, start, size = self.places[t]
        return self.arrived[array][start : start + size].astype(F32)

    def finish(self):
        return [self.home[t] + self.came(t) for t in range(2)]


def exchange(items, orders, n_row):
    groups = {}
    for item in items:
        for t in range(2):
            home, came = item.home[t], item.came(t)
            half = home.shape[0] // 2
            groups.setdefault(orders[t][item.step], []).append(
                (item, t, (home[:half] + came[:half]).astype(BF16))
            )
            item.home[t] = home[half:] + came[half:]
    arrived, sent = [], []
    for number, (b, members) in enumerate(sorted(groups.items())):
        sent.append(jnp.concatenate([rows for _, _, rows in members], axis=0))
        arrived.append(swap(sent[-1], "row", n_row, 1 << b))
        start = 0
        for item, t, rows in members:
            item.places[t] = (number, start, rows.shape[0])
            start += rows.shape[0]
    for item in items:
        item.arrived = arrived
        item.step += 1
    return sent


def finish_kernel(gate_home, gate_came, up_home, up_came, sums, gate_b, gate_c, up_b, up_c, *refs):
    rank = 2 * gate_b.shape[0]
    high = sums[...].astype(BF16)
    low = (sums[...] - high.astype(F32)).astype(BF16)

    def total(home, came, mine, other, units, columns):
        upper = jnp.concatenate([mine[:, units], other[:, units]], axis=0)
        value = home[:, units] + came[:, units].astype(F32)
        for part in (high, low):
            value += jnp.dot(part[:, columns], upper, preferred_element_type=F32)
        return value

    for start in range(0, gate_home.shape[1], TILE):
        units = slice(start, start + TILE)
        gate = total(gate_home, gate_came, gate_b, gate_c, units, slice(0, rank))
        up = total(up_home, up_came, up_b, up_c, units, slice(rank, 2 * rank))
        refs[-1][:, units] = (jax.nn.silu(gate) * up).astype(BF16)


def finished(number, item, sums, uppers, units, hidden):
    rows, columns = item.home[0].shape
    home = pl.BlockSpec((rows, columns), lambda i: (0, 0))
    upper = pl.BlockSpec((uppers[0].shape[0], columns), lambda i: (0, number))
    operands, specs = [], []
    for t in range(2):
        array, start, _ = item.places[t]
        block = start // rows
        operands += [item.home[t], item.arrived[array]]
        specs += [home, pl.BlockSpec((rows, columns), lambda i, block=block: (block, 0))]
    operands += [sums, *uppers, *hidden]
    specs += [pl.BlockSpec(sums.shape, lambda i: (0, 0))] + [upper] * 4
    specs += [pl.BlockSpec(memory_space=pl.ANY)] * len(hidden)
    return pl.pallas_call(
        finish_kernel,
        grid=(1,),
        out_shape=[jax.ShapeDtypeStruct((rows, units), BF16)],
        in_specs=specs,
        out_specs=[pl.BlockSpec((rows, columns), lambda i: (0, number))],
        input_output_aliases={9: 0} if hidden else {},
        compiler_params=pltpu.CompilerParams(vmem_limit_bytes=14 * 2**20),
        name="finish",
    )(*operands)


def body(
    n_row, n_col, tokens, gate_weight, up_weight, gate_lower, up_lower, gate_upper, up_upper,
    outgoing, incoming,
):
    old, new = outgoing[0], incoming[0]
    row, col = lax.axis_index("row"), lax.axis_index("col")
    core = bit(row, 0)
    others = list(range(1, n_row.bit_length() - 1))
    orders = [others, others[1:] + others[:1]]
    stages = len(others)
    weights = [gate_weight.T, up_weight.T]
    units = weights[0].shape[0]
    rank = gate_upper.shape[1]
    tiles = pl.cdiv(pl.cdiv(units, 2 * rank) * 2 * rank + 2 * rank, TILE)
    per = pl.cdiv(tiles, CHUNKS)
    spans = [(first, min(per, tiles - first)) for first in range(0, tiles, per)]
    turns = list(range(len(spans)))
    turns[1:] = turns[:0:-1]
    used = pl.cdiv(units, TILE)

    state, sums = {"sent": []}, {}
    col_bits = list(range(n_col.bit_length() - 1))
    def slots(near, local):
        keep, other = jnp.where(near == 0, new, old), jnp.where(near == 0, old, new)
        return keep // local, [keep % local, other % local]

    upper_owner, upper_at = slots(bit(row, 0), gate_upper.shape[0])
    lower_owner, lower_at = slots(bit(col, 0), gate_lower.shape[0])

    def slot(stack, i):
        return lax.dynamic_index_in_dim(stack, i, 0, keepdims=False)

    offsets = [0]
    gathered = [swap(tokens, "col", n_col, 1 << col_bits[-1])]
    lowers = jnp.concatenate([jnp.swapaxes(a, 1, 2) for a in (gate_lower, up_lower)], axis=1)
    lower = Factor(
        "col", n_col, col, col_bits, *[slot(lowers, i) for i in lower_at], lower_owner
    )
    uppers = [
        Factor(
            "row", n_row, row, [0] + order, *[slot(stack, i) for i in upper_at], upper_owner
        )
        for stack, order in zip((gate_upper, up_upper), orders)
    ]

    def fence(*arrivals):
        items = list(sums.values())
        values = (
            state, [f.held for f in uppers + [lower]], [item.home for item in items],
            [item.arrived for item in arrivals],
        )
        values = lax.optimization_barrier(values)
        state.update(values[0])
        for factor, held in zip(uppers + [lower], values[1]):
            factor.held = held
        for item, home in zip(items, values[2]):
            item.home = home
        for item, arrived in zip(arrivals, values[3]):
            item.arrived = arrived

    def forward(*factors):
        state["sent"] = [state["sent"], [f.step() for f in factors if f.todo]]

    def running():
        return [f for f in uppers + [lower] if f.todo]

    def step():
        items = [sums[turn] for turn in turns if turn in sums]
        ready = [
            item for i, item in enumerate(items)
            if item.step < stages and (i == 0 or items[i - 1].step > item.step)
        ]
        if ready:
            state["sent"] = exchange(ready, orders, n_row)
        return ready

    for number, b in enumerate(reversed(col_bits)):
        fence()
        parts = [state.pop("parts", tokens)] + gathered
        offsets = offsets + [o ^ (1 << b) for o in offsets]
        if number + 1 < len(col_bits):
            state["parts"] = jnp.concatenate(parts, axis=0)
            gathered = [swap(state["parts"], "col", n_col, 1 << (b - 1))]
            forward(*uppers if number == 0 else (), lower)
    tok = state["tok"] = ordered_tokens(parts, offsets, n_row, row, col, orders[0])
    fence()
    forward(*uppers, lower)
    fence()

    rows = tok.shape[0] // n_row
    columns = per * TILE
    places = [block_order(orders[0]).index(k) for k in block_order(orders[1])]

    def low_factors():
        value = lower.joined()
        half = value.shape[0] // 2
        fresh, stale = value[:half], value[half:]
        return jnp.concatenate([fresh[:rank], -stale[:rank], fresh[rank:], -stale[rank:]], axis=0)

    flying = []
    for number, turn in enumerate(turns):
        part = multiply_chunk(spans[turn], columns, weights, state["tok"], rows, places)
        state["part"] = part
        fence(*running() if number < 2 else ())
        if number == 1 or len(turns) == 1:
            while lower.todo:
                forward(lower)
            state["low"] = low_factors()
            state["part"] = multiply_lower(state["tok"], state["low"], state["part"], rows, places)
        sums[turn] = Sum(*state.pop("part"), n_row)
        if number < 2:
            forward(*running())
        if number == 0:
            fence(sums[turn])
            flying = step()
        fence()
    fence(*flying, *[sums[turn] for turn in turns[1:2]])
    flying = step()
    fence()
    while running():
        fence(*uppers)
        forward(*uppers)
    fence(*uppers)

    def by_core(value, axis):
        parts = jnp.split(value, 4, axis=axis)
        turned = [parts[i] for i in (1, 0, 3, 2)]
        return jnp.where(
            core == 0, jnp.concatenate(parts, axis=axis), jnp.concatenate(turned, axis=axis)
        )

    state["uppers"] = [part for f in uppers for part in (f.held, f.arrived[0])]
    state["low"] = by_core(state["low"], 0)
    fence()
    cuts = [0, used * 2 // 5, used * 4 // 5, used]
    state["merged"] = []
    done = 0
    for first, last in zip(cuts, cuts[1:]):
        state["merged"] = merge_span(
            (first, last - first), weights, state["low"], state["uppers"], state["merged"]
        )
        fence(*flying, *[sums[turn] for turn in turns[2:] if sums[turn].step == 0])
        flying = step()
        fence()
    while flying:
        flying = step()

    ends = sums[turns[min(1, len(turns) - 1)]].finish()
    correction = jnp.concatenate([end[:, columns - 2 * rank :] for end in ends], axis=1)
    correction = by_core(correction, 1)
    hidden = []
    for turn in turns:
        hidden = finished(turn, sums[turn], correction, state["uppers"], units, hidden)
    merged = state["merged"]
    return merged[0].T, merged[1].T, hidden[0]


def solution(mesh):
    return jax.shard_map(
        functools.partial(body, mesh.shape["row"], mesh.shape["col"]),
        mesh=mesh,
        in_specs=(
            P("col", "row"),
            P("row", "col"),
            P("row", "col"),
            P("col", "row", None),
            P("col", "row", None),
            P("row", None, "col"),
            P("row", None, "col"),
            P(),
            P(),
        ),
        out_specs=(P("row", "col"), P("row", "col"), P("row", "col")),
        check_vma=False,
    )
```

```python
import functools

import jax
import jax.numpy as jnp
from jax import lax
from jax.experimental import pallas as pl
from jax.experimental.pallas import tpu as pltpu
from jax.sharding import PartitionSpec as P

TILE = 512
SUB = 256
CHUNKS = 3
F32 = jnp.float32
BF16 = jnp.bfloat16
SMALL = pl.CostEstimate(flops=1024, bytes_accessed=1024, transcendentals=0)
COST = pl.CostEstimate(flops=2**34, bytes_accessed=2**25, transcendentals=0)
VMEM = pl.BlockSpec(memory_space=pltpu.VMEM)


def after(value, others):
    return lax.optimization_barrier((value, others))[0]


def bit(value, which):
    return (value >> which) & 1


def swap(value, axis, size, distance):
    return lax.ppermute(value, axis, [(i, i ^ distance) for i in range(size)])


def block_order(bits):
    offsets = range(0, 2 ** (len(bits) + 1), 2)
    return sorted(offsets, key=lambda k: tuple(-bit(k, b) for b in bits))


class Factor:
    def __init__(self, axis, size, index, bits, held, sent, owner):
        self.axis, self.size, self.index, self.bits = axis, size, index, bits
        self.held, self.owner = held, owner
        self.arrived = [swap(sent, axis, size, 1 << bits[0])]
        self.last = bits[0]
        self.todo = [("scatter", b) for b in bits[1:]] + [("turn", bits[-1])]
        self.todo += [("gather", b) for b in reversed(bits[:-1])]

    def chosen(self):
        mine = bit(self.index, self.last)
        return jnp.where(mine == bit(self.owner, self.last), self.held, self.arrived[0])

    def joined(self):
        low = jnp.concatenate([self.held, self.arrived[0]], axis=0)
        high = jnp.concatenate([self.arrived[0], self.held], axis=0)
        return jnp.where(bit(self.index, self.last) == 0, low, high)

    def step(self):
        kind, b = self.todo.pop(0)
        if kind == "scatter":
            value = self.chosen()
            half = value.shape[0] // 2
            mine = bit(self.index, b)
            sent = lax.dynamic_slice_in_dim(value, (1 - mine) * half, half, 0)
            self.held = lax.dynamic_slice_in_dim(value, mine * half, half, 0)
        else:
            self.held = sent = self.chosen() if kind == "turn" else self.joined()
        self.arrived = [swap(sent, self.axis, self.size, 1 << b)]
        self.last = b
        return sent


def tokens_kernel(rows, at, *refs):
    first = 0
    for ref in refs[:-1]:
        for h in range(ref.shape[0] // rows):
            start = pl.multiple_of(at[first + h] * rows, rows)
            refs[-1][pl.ds(start, rows), :] = ref[h * rows : (h + 1) * rows, :]
        first += ref.shape[0] // rows


def ordered_tokens(parts, offsets, n_row, row, col, bits):
    rows = sum(part.shape[0] for part in parts) // n_row
    blocks = n_row // len(offsets)
    source = (col ^ jnp.array(offsets, jnp.int32))[:, None]
    offset = ((source * blocks + jnp.arange(blocks, dtype=jnp.int32)) ^ row).reshape(-1)
    place = offset * 0
    for b in [0] + bits:
        place = place * 2 + 1 - bit(offset, b)
    return pl.pallas_call(
        functools.partial(tokens_kernel, rows),
        out_shape=jax.ShapeDtypeStruct((rows * n_row, parts[0].shape[1]), BF16),
        in_specs=[pl.BlockSpec(memory_space=pltpu.SMEM)] + [VMEM] * len(parts),
        out_specs=VMEM,
        compiler_params=pltpu.CompilerParams(vmem_limit_bytes=12 * 2**20),
        name="order_tokens",
    )(place, *parts)


def times_transposed(left, right):
    return lax.dot_general(left, right, (((1,), (1,)), ((), ())), preferred_element_type=F32)


def multiply_kernel(rows, places, tok, gate_w, up_w, away, gate_home, up_home):
    half = tok.shape[0] // 2
    part = times_transposed(tok[...], gate_w[...])
    away[:half, :] = part[:half].astype(BF16)
    gate_home[...] = part[half:]
    part = times_transposed(tok[...], up_w[...])
    for to, at in enumerate(places):
        into = slice(to * rows, (to + 1) * rows)
        away[half + to * rows : half + (to + 1) * rows, :] = part[at * rows :][:rows].astype(BF16)
        up_home[into, :] = part[half + at * rows :][:rows]


def multiply_chunk(span, columns, weights, tok, rows, places):
    first, count = span
    n_tok, depth = tok.shape
    half = n_tok // 2
    weight = pl.BlockSpec((TILE, depth), lambda i: (first + i, 0))
    return pl.pallas_call(
        functools.partial(multiply_kernel, rows, places),
        grid=(count,),
        out_shape=[
            jax.ShapeDtypeStruct((n_tok, columns), BF16),
            jax.ShapeDtypeStruct((half, columns), F32),
            jax.ShapeDtypeStruct((half, columns), F32),
        ],
        in_specs=[pl.BlockSpec(tok.shape, lambda i: (0, 0)), weight, weight],
        out_specs=[
            pl.BlockSpec((n_tok, TILE), lambda i: (0, i)),
            pl.BlockSpec((half, TILE), lambda i: (0, i)),
            pl.BlockSpec((half, TILE), lambda i: (0, i)),
        ],
        compiler_params=pltpu.CompilerParams(
            dimension_semantics=("arbitrary",), vmem_limit_bytes=40 * 2**20
        ),
        cost_estimate=COST,
        name="multiply",
    )(tok, *weights)


def lower_kernel(rows, places, tok, low, old_away, old_gate, old_up, away, gate_home, up_home):
    rank = low.shape[0] // 2
    multiply_kernel(
        rows, places, tok, low.at[:rank, :], low.at[rank:, :], away, gate_home, up_home
    )


def multiply_lower(tok, low, part, rows, places):
    rank = low.shape[0] // 2
    last = part[0].shape[1] // rank - 1
    specs = [pl.BlockSpec((array.shape[0], rank), lambda i: (0, last)) for array in part]
    return pl.pallas_call(
        functools.partial(lower_kernel, rows, places),
        grid=(1,),
        out_shape=[jax.ShapeDtypeStruct(array.shape, array.dtype) for array in part],
        in_specs=[pl.BlockSpec(array.shape, lambda i: (0, 0)) for array in (tok, low)] + specs,
        out_specs=specs,
        input_output_aliases={2: 0, 3: 1, 4: 2},
        compiler_params=pltpu.CompilerParams(vmem_limit_bytes=12 * 2**20),
        cost_estimate=SMALL,
        name="multiply_lower",
    )(tok, low, *part)


def merge_kernel(low, gate_w, up_w, gate_b, gate_c, up_b, up_c, *refs):
    rank = gate_b.shape[0]
    for start in range(0, TILE, SUB):
        units = slice(start, start + SUB)
        for t, (weight, mine, other) in enumerate(
            ((gate_w, gate_b, gate_c), (up_w, up_b, up_c))
        ):
            delta = lax.dot_general(
                jnp.concatenate([mine[:, units], other[:, units]], axis=0),
                low[2 * t * rank : 2 * (t + 1) * rank, :],
                (((0,), (0,)), ((), ())),
                preferred_element_type=F32,
            )
            refs[t - 2][units, :] = (weight[units, :].astype(F32) + delta).astype(BF16)


def merge_span(span, weights, low, uppers, merged):
    first, count = span
    units, depth = weights[0].shape
    weight = pl.BlockSpec((TILE, depth), lambda i: (first + i, 0))
    upper = pl.BlockSpec((uppers[0].shape[0], TILE), lambda i: (0, first + i))
    operands = [low, *weights, *uppers, *merged]
    specs = [pl.BlockSpec(low.shape, lambda i: (0, 0)), weight, weight] + [upper] * 4
    specs += [pl.BlockSpec(memory_space=pl.ANY)] * len(merged)
    return pl.pallas_call(
        merge_kernel,
        grid=(count,),
        out_shape=[jax.ShapeDtypeStruct((units, depth), BF16)] * 2,
        in_specs=specs,
        out_specs=[weight] * 2,
        input_output_aliases={7: 0, 8: 1} if merged else {},
        compiler_params=pltpu.CompilerParams(
            dimension_semantics=("arbitrary",), vmem_limit_bytes=40 * 2**20
        ),
        cost_estimate=SMALL,
        name="merge",
    )(*operands)


class Sum:
    def __init__(self, away, gate, up, n_row):
        half = gate.shape[0]
        self.home = [gate, up]
        self.arrived = [swap(away, "row", n_row, 1)]
        self.places = [(0, 0, half), (0, half, half)]
        self.step = 0

    def came(self, t):
        array, start, size = self.places[t]
        return self.arrived[array][start : start + size].astype(F32)

    def finish(self):
        return [self.home[t] + self.came(t) for t in range(2)]


def exchange(items, orders, n_row):
    groups = {}
    for item in items:
        for t in range(2):
            home, came = item.home[t], item.came(t)
            half = home.shape[0] // 2
            groups.setdefault(orders[t][item.step], []).append(
                (item, t, (home[:half] + came[:half]).astype(BF16))
            )
            item.home[t] = home[half:] + came[half:]
    arrived, sent = [], []
    for number, (b, members) in enumerate(sorted(groups.items())):
        sent.append(jnp.concatenate([rows for _, _, rows in members], axis=0))
        arrived.append(swap(sent[-1], "row", n_row, 1 << b))
        start = 0
        for item, t, rows in members:
            item.places[t] = (number, start, rows.shape[0])
            start += rows.shape[0]
    for item in items:
        item.arrived = arrived
        item.step += 1
    return sent


def finish_kernel(gate_home, gate_came, up_home, up_came, sums, gate_b, gate_c, up_b, up_c, *refs):
    rank = 2 * gate_b.shape[0]
    high = sums[...].astype(BF16)
    low = (sums[...] - high.astype(F32)).astype(BF16)

    def total(home, came, mine, other, units, columns):
        upper = jnp.concatenate([mine[:, units], other[:, units]], axis=0)
        value = home[:, units] + came[:, units].astype(F32)
        for part in (high, low):
            value += jnp.dot(part[:, columns], upper, preferred_element_type=F32)
        return value

    for start in range(0, gate_home.shape[1], TILE):
        units = slice(start, start + TILE)
        gate = total(gate_home, gate_came, gate_b, gate_c, units, slice(0, rank))
        up = total(up_home, up_came, up_b, up_c, units, slice(rank, 2 * rank))
        refs[-1][:, units] = (jax.nn.silu(gate) * up).astype(BF16)


def finished(number, item, sums, uppers, units, hidden):
    rows, columns = item.home[0].shape
    home = pl.BlockSpec((rows, columns), lambda i: (0, 0))
    upper = pl.BlockSpec((uppers[0].shape[0], columns), lambda i: (0, number))
    operands, specs = [], []
    for t in range(2):
        array, start, _ = item.places[t]
        block = start // rows
        operands += [item.home[t], item.arrived[array]]
        specs += [home, pl.BlockSpec((rows, columns), lambda i, block=block: (block, 0))]
    operands += [sums, *uppers, *hidden]
    specs += [pl.BlockSpec(sums.shape, lambda i: (0, 0))] + [upper] * 4
    specs += [pl.BlockSpec(memory_space=pl.ANY)] * len(hidden)
    return pl.pallas_call(
        finish_kernel,
        grid=(1,),
        out_shape=[jax.ShapeDtypeStruct((rows, units), BF16)],
        in_specs=specs,
        out_specs=[pl.BlockSpec((rows, columns), lambda i: (0, number))],
        input_output_aliases={9: 0} if hidden else {},
        compiler_params=pltpu.CompilerParams(vmem_limit_bytes=14 * 2**20),
        name="finish",
    )(*operands)


def body(
    n_row, n_col, tokens, gate_weight, up_weight, gate_lower, up_lower, gate_upper, up_upper,
    outgoing, incoming,
):
    old, new = outgoing[0], incoming[0]
    row, col = lax.axis_index("row"), lax.axis_index("col")
    core = bit(row, 0)
    others = list(range(1, n_row.bit_length() - 1))
    orders = [others, others[1:] + others[:1]]
    stages = len(others)
    weights = [gate_weight.T, up_weight.T]
    units = weights[0].shape[0]
    rank = gate_upper.shape[1]
    tiles = pl.cdiv(pl.cdiv(units, 2 * rank) * 2 * rank + 2 * rank, TILE)
    per = pl.cdiv(tiles, CHUNKS)
    spans = [(first, min(per, tiles - first)) for first in range(0, tiles, per)]
    turns = list(range(len(spans)))
    turns[1:] = turns[:0:-1]
    used = pl.cdiv(units, TILE)

    state, sums = {"sent": []}, {}
    col_bits = list(range(n_col.bit_length() - 1))
    def slots(near, local):
        keep, other = jnp.where(near == 0, new, old), jnp.where(near == 0, old, new)
        return keep // local, [keep % local, other % local]

    upper_owner, upper_at = slots(bit(row, 0), gate_upper.shape[0])
    lower_owner, lower_at = slots(bit(col, 0), gate_lower.shape[0])

    def slot(stack, i):
        return lax.dynamic_index_in_dim(stack, i, 0, keepdims=False)

    offsets = [0]
    gathered = [swap(tokens, "col", n_col, 1 << col_bits[-1])]
    lowers = jnp.concatenate([jnp.swapaxes(a, 1, 2) for a in (gate_lower, up_lower)], axis=1)
    lower = Factor(
        "col", n_col, col, col_bits, *[slot(lowers, i) for i in lower_at], lower_owner
    )
    uppers = [
        Factor(
            "row", n_row, row, [0] + order, *[slot(stack, i) for i in upper_at], upper_owner
        )
        for stack, order in zip((gate_upper, up_upper), orders)
    ]

    def fence(*arrivals):
        items = list(sums.values())
        values = (
            state, [f.held for f in uppers + [lower]], [item.home for item in items],
            [item.arrived for item in arrivals],
        )
        values = lax.optimization_barrier(values)
        state.update(values[0])
        for factor, held in zip(uppers + [lower], values[1]):
            factor.held = held
        for item, home in zip(items, values[2]):
            item.home = home
        for item, arrived in zip(arrivals, values[3]):
            item.arrived = arrived

    def forward(*factors):
        state["sent"] = [state["sent"], [f.step() for f in factors if f.todo]]

    def running():
        return [f for f in uppers + [lower] if f.todo]

    def step():
        items = [sums[turn] for turn in turns if turn in sums]
        ready = [
            item for i, item in enumerate(items)
            if item.step < stages and (i == 0 or items[i - 1].step > item.step)
        ]
        if ready:
            state["sent"] = exchange(ready, orders, n_row)
        return ready

    for number, b in enumerate(reversed(col_bits)):
        fence()
        parts = [state.pop("parts", tokens)] + gathered
        offsets = offsets + [o ^ (1 << b) for o in offsets]
        if number + 1 < len(col_bits):
            state["parts"] = jnp.concatenate(parts, axis=0)
            gathered = [swap(state["parts"], "col", n_col, 1 << (b - 1))]
            forward(*uppers if number == 0 else (), lower)
    tok = state["tok"] = ordered_tokens(parts, offsets, n_row, row, col, orders[0])
    fence()
    forward(*uppers, lower)
    fence()

    rows = tok.shape[0] // n_row
    columns = per * TILE
    places = [block_order(orders[0]).index(k) for k in block_order(orders[1])]

    def low_factors():
        value = lower.joined()
        half = value.shape[0] // 2
        fresh, stale = value[:half], value[half:]
        return jnp.concatenate([fresh[:rank], -stale[:rank], fresh[rank:], -stale[rank:]], axis=0)

    flying = []
    for number, turn in enumerate(turns):
        part = multiply_chunk(spans[turn], columns, weights, state["tok"], rows, places)
        state["part"] = part
        fence(*running() if number < 2 else ())
        if number == 1 or len(turns) == 1:
            while lower.todo:
                forward(lower)
            state["low"] = low_factors()
            state["part"] = multiply_lower(state["tok"], state["low"], state["part"], rows, places)
        sums[turn] = Sum(*state.pop("part"), n_row)
        if number < 2:
            forward(*running())
        if number == 0:
            fence(sums[turn])
            flying = step()
        fence()
    fence(*flying, *[sums[turn] for turn in turns[1:2]])
    flying = step()
    fence()
    while running():
        fence(*uppers)
        forward(*uppers)
    fence(*uppers)

    def by_core(value, axis):
        parts = jnp.split(value, 4, axis=axis)
        turned = [parts[i] for i in (1, 0, 3, 2)]
        return jnp.where(
            core == 0, jnp.concatenate(parts, axis=axis), jnp.concatenate(turned, axis=axis)
        )

    state["uppers"] = [part for f in uppers for part in (f.held, f.arrived[0])]
    state["low"] = by_core(state["low"], 0)
    fence()
    small = pl.cdiv(used, 16)
    cuts = [0, (used - small + 1) // 2, used - small, used]
    def finish(chosen, hidden):
        if chosen and "correction" not in state:
            ends = sums[turns[min(1, len(turns) - 1)]].finish()
            correction = jnp.concatenate([end[:, columns - 2 * rank :] for end in ends], axis=1)
            state["correction"] = by_core(correction, 1)
        for turn in chosen:
            hidden = finished(turn, sums[turn], state["correction"], state["uppers"], units, hidden)
        return hidden

    state["merged"] = []
    for first, last in zip(cuts, cuts[1:]):
        state["merged"] = merge_span(
            (first, last - first), weights, state["low"], state["uppers"], state["merged"]
        )
        if last == used:
            early = [t for t in turns[:-1] if all(sums[i].step == stages for i in turns[:-1])]
            state["hidden"] = finish(early, [])
        fence(*flying, *[sums[turn] for turn in turns[2:] if sums[turn].step == 0])
        flying = step()
        fence()
    while flying:
        flying = step()
    hidden = finish([turn for turn in turns if turn not in early], state["hidden"])
    merged = state["merged"]
    return merged[0].T, merged[1].T, hidden[0]


def solution(mesh):
    return jax.shard_map(
        functools.partial(body, mesh.shape["row"], mesh.shape["col"]),
        mesh=mesh,
        in_specs=(
            P("col", "row"),
            P("row", "col"),
            P("row", "col"),
            P("col", "row", None),
            P("col", "row", None),
            P("row", None, "col"),
            P("row", None, "col"),
            P(),
            P(),
        ),
        out_specs=(P("row", "col"), P("row", "col"), P("row", "col")),
        check_vma=False,
    )
```

```python
import functools

import jax
import jax.numpy as jnp
from jax import lax
from jax.experimental import pallas as pl
from jax.experimental.pallas import tpu as pltpu
from jax.sharding import PartitionSpec as P

TILE = 512
SUB = 256
CHUNKS = 3
F32 = jnp.float32
BF16 = jnp.bfloat16
SMALL = pl.CostEstimate(flops=1024, bytes_accessed=1024, transcendentals=0)
COST = pl.CostEstimate(flops=2**34, bytes_accessed=2**25, transcendentals=0)
VMEM = pl.BlockSpec(memory_space=pltpu.VMEM)


def after(value, others):
    return lax.optimization_barrier((value, others))[0]


def bit(value, which):
    return (value >> which) & 1


def swap(value, axis, size, distance):
    return lax.ppermute(value, axis, [(i, i ^ distance) for i in range(size)])


def block_order(bits):
    offsets = range(0, 2 ** (len(bits) + 1), 2)
    return sorted(offsets, key=lambda k: tuple(-bit(k, b) for b in bits))


class Factor:
    def __init__(self, axis, size, index, bits, held, sent, owner):
        self.axis, self.size, self.index, self.bits = axis, size, index, bits
        self.held, self.owner = held, owner
        self.arrived = [swap(sent, axis, size, 1 << bits[0])]
        self.last = bits[0]
        self.todo = [("scatter", b) for b in bits[1:]] + [("turn", bits[-1])]
        self.todo += [("gather", b) for b in reversed(bits[:-1])]

    def chosen(self):
        mine = bit(self.index, self.last)
        return jnp.where(mine == bit(self.owner, self.last), self.held, self.arrived[0])

    def joined(self):
        low = jnp.concatenate([self.held, self.arrived[0]], axis=0)
        high = jnp.concatenate([self.arrived[0], self.held], axis=0)
        return jnp.where(bit(self.index, self.last) == 0, low, high)

    def step(self):
        kind, b = self.todo.pop(0)
        if kind == "scatter":
            value = self.chosen()
            half = value.shape[0] // 2
            mine = bit(self.index, b)
            sent = lax.dynamic_slice_in_dim(value, (1 - mine) * half, half, 0)
            self.held = lax.dynamic_slice_in_dim(value, mine * half, half, 0)
        else:
            self.held = sent = self.chosen() if kind == "turn" else self.joined()
        self.arrived = [swap(sent, self.axis, self.size, 1 << b)]
        self.last = b
        return sent


def tokens_kernel(rows, at, *refs):
    first = 0
    for ref in refs[:-1]:
        for h in range(ref.shape[0] // rows):
            start = pl.multiple_of(at[first + h] * rows, rows)
            refs[-1][pl.ds(start, rows), :] = ref[h * rows : (h + 1) * rows, :]
        first += ref.shape[0] // rows


def ordered_tokens(parts, offsets, n_row, row, col, bits):
    rows = sum(part.shape[0] for part in parts) // n_row
    blocks = n_row // len(offsets)
    source = (col ^ jnp.array(offsets, jnp.int32))[:, None]
    offset = ((source * blocks + jnp.arange(blocks, dtype=jnp.int32)) ^ row).reshape(-1)
    place = offset * 0
    for b in [0] + bits:
        place = place * 2 + 1 - bit(offset, b)
    return pl.pallas_call(
        functools.partial(tokens_kernel, rows),
        out_shape=jax.ShapeDtypeStruct((rows * n_row, parts[0].shape[1]), BF16),
        in_specs=[pl.BlockSpec(memory_space=pltpu.SMEM)] + [VMEM] * len(parts),
        out_specs=VMEM,
        compiler_params=pltpu.CompilerParams(vmem_limit_bytes=12 * 2**20),
        name="order_tokens",
    )(place, *parts)


def times_transposed(left, right):
    return lax.dot_general(left, right, (((1,), (1,)), ((), ())), preferred_element_type=F32)


def multiply_kernel(rows, places, tok, gate_w, up_w, away, gate_home, up_home):
    half = tok.shape[0] // 2
    part = times_transposed(tok[...], gate_w[...])
    away[:half, :] = part[:half].astype(BF16)
    gate_home[...] = part[half:]
    part = times_transposed(tok[...], up_w[...])
    for to, at in enumerate(places):
        into = slice(to * rows, (to + 1) * rows)
        away[half + to * rows : half + (to + 1) * rows, :] = part[at * rows :][:rows].astype(BF16)
        up_home[into, :] = part[half + at * rows :][:rows]


def multiply_chunk(span, columns, weights, tok, rows, places):
    first, count = span
    n_tok, depth = tok.shape
    half = n_tok // 2
    weight = pl.BlockSpec((TILE, depth), lambda i: (first + i, 0))
    return pl.pallas_call(
        functools.partial(multiply_kernel, rows, places),
        grid=(count,),
        out_shape=[
            jax.ShapeDtypeStruct((n_tok, columns), BF16),
            jax.ShapeDtypeStruct((half, columns), F32),
            jax.ShapeDtypeStruct((half, columns), F32),
        ],
        in_specs=[pl.BlockSpec(tok.shape, lambda i: (0, 0)), weight, weight],
        out_specs=[
            pl.BlockSpec((n_tok, TILE), lambda i: (0, i)),
            pl.BlockSpec((half, TILE), lambda i: (0, i)),
            pl.BlockSpec((half, TILE), lambda i: (0, i)),
        ],
        compiler_params=pltpu.CompilerParams(
            dimension_semantics=("arbitrary",), vmem_limit_bytes=22 * 2**20
        ),
        cost_estimate=COST,
        name="multiply",
    )(tok, *weights)


def lower_kernel(rows, places, tok, low, old_away, old_gate, old_up, away, gate_home, up_home):
    rank = low.shape[0] // 2
    multiply_kernel(
        rows, places, tok, low.at[:rank, :], low.at[rank:, :], away, gate_home, up_home
    )


def multiply_lower(tok, low, part, rows, places):
    rank = low.shape[0] // 2
    last = part[0].shape[1] // rank - 1
    specs = [pl.BlockSpec((array.shape[0], rank), lambda i: (0, last)) for array in part]
    return pl.pallas_call(
        functools.partial(lower_kernel, rows, places),
        grid=(1,),
        out_shape=[jax.ShapeDtypeStruct(array.shape, array.dtype) for array in part],
        in_specs=[pl.BlockSpec(array.shape, lambda i: (0, 0)) for array in (tok, low)] + specs,
        out_specs=specs,
        input_output_aliases={2: 0, 3: 1, 4: 2},
        compiler_params=pltpu.CompilerParams(vmem_limit_bytes=12 * 2**20),
        cost_estimate=SMALL,
        name="multiply_lower",
    )(tok, low, *part)


def merge_kernel(low, gate_w, up_w, gate_b, gate_c, up_b, up_c, *refs):
    rank = gate_b.shape[0]
    for start in range(0, TILE, SUB):
        units = slice(start, start + SUB)
        for t, (weight, mine, other) in enumerate(
            ((gate_w, gate_b, gate_c), (up_w, up_b, up_c))
        ):
            delta = lax.dot_general(
                jnp.concatenate([mine[:, units], other[:, units]], axis=0),
                low[2 * t * rank : 2 * (t + 1) * rank, :],
                (((0,), (0,)), ((), ())),
                preferred_element_type=F32,
            )
            refs[t - 2][units, :] = (weight[units, :].astype(F32) + delta).astype(BF16)


def merge_span(span, weights, low, uppers, merged):
    first, count = span
    units, depth = weights[0].shape
    weight = pl.BlockSpec((TILE, depth), lambda i: (first + i, 0))
    upper = pl.BlockSpec((uppers[0].shape[0], TILE), lambda i: (0, first + i))
    operands = [low, *weights, *uppers, *merged]
    specs = [pl.BlockSpec(low.shape, lambda i: (0, 0)), weight, weight] + [upper] * 4
    specs += [pl.BlockSpec(memory_space=pl.ANY)] * len(merged)
    return pl.pallas_call(
        merge_kernel,
        grid=(count,),
        out_shape=[jax.ShapeDtypeStruct((units, depth), BF16)] * 2,
        in_specs=specs,
        out_specs=[weight] * 2,
        input_output_aliases={7: 0, 8: 1} if merged else {},
        compiler_params=pltpu.CompilerParams(
            dimension_semantics=("arbitrary",), vmem_limit_bytes=22 * 2**20
        ),
        cost_estimate=SMALL,
        name="merge",
    )(*operands)


class Sum:
    def __init__(self, away, gate, up, n_row):
        half = gate.shape[0]
        self.home = [gate, up]
        self.arrived = [swap(away, "row", n_row, 1)]
        self.places = [(0, 0, half), (0, half, half)]
        self.step = 0

    def came(self, t):
        array, start, size = self.places[t]
        return self.arrived[array][start : start + size].astype(F32)

    def finish(self):
        return [self.home[t] + self.came(t) for t in range(2)]


def exchange(items, orders, n_row):
    groups = {}
    for item in items:
        for t in range(2):
            home, came = item.home[t], item.came(t)
            half = home.shape[0] // 2
            groups.setdefault(orders[t][item.step], []).append(
                (item, t, (home[:half] + came[:half]).astype(BF16))
            )
            item.home[t] = home[half:] + came[half:]
    arrived, sent = [], []
    for number, (b, members) in enumerate(sorted(groups.items())):
        sent.append(jnp.concatenate([rows for _, _, rows in members], axis=0))
        arrived.append(swap(sent[-1], "row", n_row, 1 << b))
        start = 0
        for item, t, rows in members:
            item.places[t] = (number, start, rows.shape[0])
            start += rows.shape[0]
    for item in items:
        item.arrived = arrived
        item.step += 1
    return sent


def finish_kernel(gate_home, gate_came, up_home, up_came, sums, gate_b, gate_c, up_b, up_c, *refs):
    rank = 2 * gate_b.shape[0]
    high = sums[...].astype(BF16)
    low = (sums[...] - high.astype(F32)).astype(BF16)

    def total(home, came, mine, other, units, columns):
        upper = jnp.concatenate([mine[:, units], other[:, units]], axis=0)
        value = home[:, units] + came[:, units].astype(F32)
        for part in (high, low):
            value += jnp.dot(part[:, columns], upper, preferred_element_type=F32)
        return value

    for start in range(0, gate_home.shape[1], TILE):
        units = slice(start, start + TILE)
        gate = total(gate_home, gate_came, gate_b, gate_c, units, slice(0, rank))
        up = total(up_home, up_came, up_b, up_c, units, slice(rank, 2 * rank))
        refs[-1][:, units] = (jax.nn.silu(gate) * up).astype(BF16)


def finished(number, item, sums, uppers, units, hidden):
    rows, columns = item.home[0].shape
    home = pl.BlockSpec((rows, columns), lambda i: (0, 0))
    upper = pl.BlockSpec((uppers[0].shape[0], columns), lambda i: (0, number))
    operands, specs = [], []
    for t in range(2):
        array, start, _ = item.places[t]
        block = start // rows
        operands += [item.home[t], item.arrived[array]]
        specs += [home, pl.BlockSpec((rows, columns), lambda i, block=block: (block, 0))]
    operands += [sums, *uppers, *hidden]
    specs += [pl.BlockSpec(sums.shape, lambda i: (0, 0))] + [upper] * 4
    specs += [pl.BlockSpec(memory_space=pl.ANY)] * len(hidden)
    return pl.pallas_call(
        finish_kernel,
        grid=(1,),
        out_shape=[jax.ShapeDtypeStruct((rows, units), BF16)],
        in_specs=specs,
        out_specs=[pl.BlockSpec((rows, columns), lambda i: (0, number))],
        input_output_aliases={9: 0} if hidden else {},
        compiler_params=pltpu.CompilerParams(vmem_limit_bytes=14 * 2**20),
        name="finish",
    )(*operands)


def body(
    n_row, n_col, tokens, gate_weight, up_weight, gate_lower, up_lower, gate_upper, up_upper,
    outgoing, incoming,
):
    old, new = outgoing[0], incoming[0]
    row, col = lax.axis_index("row"), lax.axis_index("col")
    core = bit(row, 0)
    others = list(range(1, n_row.bit_length() - 1))
    orders = [others, others[1:] + others[:1]]
    stages = len(others)
    weights = [gate_weight.T, up_weight.T]
    units = weights[0].shape[0]
    rank = gate_upper.shape[1]
    tiles = pl.cdiv(pl.cdiv(units, 2 * rank) * 2 * rank + 2 * rank, TILE)
    per = pl.cdiv(tiles, CHUNKS)
    spans = [(first, min(per, tiles - first)) for first in range(0, tiles, per)]
    turns = list(range(len(spans)))
    turns[1:] = turns[:0:-1]
    used = pl.cdiv(units, TILE)

    state, sums = {"sent": []}, {}
    col_bits = list(range(n_col.bit_length() - 1))
    def slots(near, local):
        keep, other = jnp.where(near == 0, new, old), jnp.where(near == 0, old, new)
        return keep // local, [keep % local, other % local]

    upper_owner, upper_at = slots(bit(row, 0), gate_upper.shape[0])
    lower_owner, lower_at = slots(bit(col, 0), gate_lower.shape[0])

    def slot(stack, i):
        return lax.dynamic_index_in_dim(stack, i, 0, keepdims=False)

    offsets = [0]
    gathered = [swap(tokens, "col", n_col, 1 << col_bits[-1])]
    lowers = jnp.concatenate([jnp.swapaxes(a, 1, 2) for a in (gate_lower, up_lower)], axis=1)
    lower = Factor(
        "col", n_col, col, col_bits, *[slot(lowers, i) for i in lower_at], lower_owner
    )
    uppers = [
        Factor(
            "row", n_row, row, [0] + order, *[slot(stack, i) for i in upper_at], upper_owner
        )
        for stack, order in zip((gate_upper, up_upper), orders)
    ]

    def fence(*arrivals):
        items = list(sums.values())
        values = (
            state, [f.held for f in uppers + [lower]], [item.home for item in items],
            [item.arrived for item in arrivals],
        )
        values = lax.optimization_barrier(values)
        state.update(values[0])
        for factor, held in zip(uppers + [lower], values[1]):
            factor.held = held
        for item, home in zip(items, values[2]):
            item.home = home
        for item, arrived in zip(arrivals, values[3]):
            item.arrived = arrived

    def forward(*factors):
        state["sent"] = [state["sent"], [f.step() for f in factors if f.todo]]

    def running():
        return [f for f in uppers + [lower] if f.todo]

    def step():
        items = [sums[turn] for turn in turns if turn in sums]
        ready = [
            item for i, item in enumerate(items)
            if item.step < stages and (i == 0 or items[i - 1].step > item.step)
        ]
        if ready:
            state["sent"] = exchange(ready, orders, n_row)
        return ready

    for number, b in enumerate(reversed(col_bits)):
        fence()
        parts = [state.pop("parts", tokens)] + gathered
        offsets = offsets + [o ^ (1 << b) for o in offsets]
        if number + 1 < len(col_bits):
            state["parts"] = jnp.concatenate(parts, axis=0)
            gathered = [swap(state["parts"], "col", n_col, 1 << (b - 1))]
            forward(*uppers if number == 0 else (), lower)
    tok = state["tok"] = ordered_tokens(parts, offsets, n_row, row, col, orders[0])
    fence()
    forward(*uppers, lower)
    fence()

    rows = tok.shape[0] // n_row
    columns = per * TILE
    places = [block_order(orders[0]).index(k) for k in block_order(orders[1])]

    def low_factors():
        value = lower.joined()
        half = value.shape[0] // 2
        fresh, stale = value[:half], value[half:]
        return jnp.concatenate([fresh[:rank], -stale[:rank], fresh[rank:], -stale[rank:]], axis=0)

    flying = []
    for number, turn in enumerate(turns):
        part = multiply_chunk(spans[turn], columns, weights, state["tok"], rows, places)
        state["part"] = part
        fence(*running() if number < 2 else ())
        if number == 1 or len(turns) == 1:
            while lower.todo:
                forward(lower)
            state["low"] = low_factors()
            state["part"] = multiply_lower(state["tok"], state["low"], state["part"], rows, places)
        sums[turn] = Sum(*state.pop("part"), n_row)
        if number < 2:
            forward(*running())
        if number == 0:
            fence(sums[turn])
            flying = step()
        fence()
    fence(*flying, *[sums[turn] for turn in turns[1:2]])
    flying = step()
    fence()
    while running():
        fence(*uppers)
        forward(*uppers)
    fence(*uppers)

    def by_core(value, axis):
        parts = jnp.split(value, 4, axis=axis)
        turned = [parts[i] for i in (1, 0, 3, 2)]
        return jnp.where(
            core == 0, jnp.concatenate(parts, axis=axis), jnp.concatenate(turned, axis=axis)
        )

    state["uppers"] = [part for f in uppers for part in (f.held, f.arrived[0])]
    state["low"] = by_core(state["low"], 0)
    fence()
    small = pl.cdiv(used, 16)
    cuts = [0, (used - small + 1) // 2, used - small, used]
    def finish(chosen, hidden):
        if chosen and "correction" not in state:
            ends = sums[turns[min(1, len(turns) - 1)]].finish()
            correction = jnp.concatenate([end[:, columns - 2 * rank :] for end in ends], axis=1)
            state["correction"] = by_core(correction, 1)
        for turn in chosen:
            hidden = finished(turn, sums[turn], state["correction"], state["uppers"], units, hidden)
        return hidden

    state["merged"] = []
    for first, last in zip(cuts, cuts[1:]):
        state["merged"] = merge_span(
            (first, last - first), weights, state["low"], state["uppers"], state["merged"]
        )
        if last == used:
            early = [t for t in turns[:-1] if all(sums[i].step == stages for i in turns[:-1])]
            state["hidden"] = finish(early, [])
        fence(*flying, *[sums[turn] for turn in turns[2:] if sums[turn].step == 0])
        flying = step()
        fence()
    while flying:
        flying = step()
    hidden = finish([turn for turn in turns if turn not in early], state["hidden"])
    merged = state["merged"]
    return merged[0].T, merged[1].T, hidden[0]


def solution(mesh):
    return jax.shard_map(
        functools.partial(body, mesh.shape["row"], mesh.shape["col"]),
        mesh=mesh,
        in_specs=(
            P("col", "row"),
            P("row", "col"),
            P("row", "col"),
            P("col", "row", None),
            P("col", "row", None),
            P("row", None, "col"),
            P("row", None, "col"),
            P(),
            P(),
        ),
        out_specs=(P("row", "col"), P("row", "col"), P("row", "col")),
        check_vma=False,
    )
```

```python
import functools

import jax
import jax.numpy as jnp
from jax import lax
from jax.experimental import pallas as pl
from jax.experimental.pallas import tpu as pltpu
from jax.sharding import PartitionSpec as P

TILE = 512
SUB = 256
CHUNKS = 3
F32 = jnp.float32
BF16 = jnp.bfloat16
SMALL = pl.CostEstimate(flops=1024, bytes_accessed=1024, transcendentals=0)
COST = pl.CostEstimate(flops=2**34, bytes_accessed=2**25, transcendentals=0)
VMEM = pl.BlockSpec(memory_space=pltpu.VMEM)


def after(value, others):
    return lax.optimization_barrier((value, others))[0]


def bit(value, which):
    return (value >> which) & 1


def swap(value, axis, size, distance):
    return lax.ppermute(value, axis, [(i, i ^ distance) for i in range(size)])


def block_order(bits):
    offsets = range(0, 2 ** (len(bits) + 1), 2)
    return sorted(offsets, key=lambda k: tuple(-bit(k, b) for b in bits))


class Factor:
    def __init__(self, axis, size, index, bits, held, sent, owner):
        self.axis, self.size, self.index, self.bits = axis, size, index, bits
        self.held, self.owner = held, owner
        self.arrived = [swap(sent, axis, size, 1 << bits[0])]
        self.last = bits[0]
        self.todo = [("scatter", b) for b in bits[1:]] + [("turn", bits[-1])]
        self.todo += [("gather", b) for b in reversed(bits[:-1])]

    def chosen(self):
        mine = bit(self.index, self.last)
        return jnp.where(mine == bit(self.owner, self.last), self.held, self.arrived[0])

    def joined(self):
        low = jnp.concatenate([self.held, self.arrived[0]], axis=0)
        high = jnp.concatenate([self.arrived[0], self.held], axis=0)
        return jnp.where(bit(self.index, self.last) == 0, low, high)

    def step(self):
        kind, b = self.todo.pop(0)
        if kind == "scatter":
            value = self.chosen()
            half = value.shape[0] // 2
            mine = bit(self.index, b)
            sent = lax.dynamic_slice_in_dim(value, (1 - mine) * half, half, 0)
            self.held = lax.dynamic_slice_in_dim(value, mine * half, half, 0)
        else:
            self.held = sent = self.chosen() if kind == "turn" else self.joined()
        self.arrived = [swap(sent, self.axis, self.size, 1 << b)]
        self.last = b
        return sent


def tokens_kernel(rows, at, *refs):
    first = 0
    for ref in refs[:-1]:
        for h in range(ref.shape[0] // rows):
            start = pl.multiple_of(at[first + h] * rows, rows)
            refs[-1][pl.ds(start, rows), :] = ref[h * rows : (h + 1) * rows, :]
        first += ref.shape[0] // rows


def ordered_tokens(parts, offsets, n_row, row, col, bits):
    rows = sum(part.shape[0] for part in parts) // n_row
    blocks = n_row // len(offsets)
    source = (col ^ jnp.array(offsets, jnp.int32))[:, None]
    offset = ((source * blocks + jnp.arange(blocks, dtype=jnp.int32)) ^ row).reshape(-1)
    place = offset * 0
    for b in [0] + bits:
        place = place * 2 + 1 - bit(offset, b)
    return pl.pallas_call(
        functools.partial(tokens_kernel, rows),
        out_shape=jax.ShapeDtypeStruct((rows * n_row, parts[0].shape[1]), BF16),
        in_specs=[pl.BlockSpec(memory_space=pltpu.SMEM)] + [VMEM] * len(parts),
        out_specs=VMEM,
        compiler_params=pltpu.CompilerParams(vmem_limit_bytes=12 * 2**20),
        name="order_tokens",
    )(place, *parts)


def times_transposed(left, right):
    return lax.dot_general(left, right, (((1,), (1,)), ((), ())), preferred_element_type=F32)


def multiply_kernel(rows, places, tok, gate_w, up_w, away, gate_home, up_home):
    half = tok.shape[0] // 2
    part = times_transposed(tok[...], gate_w[...])
    away[:half, :] = part[:half].astype(BF16)
    gate_home[...] = part[half:]
    part = times_transposed(tok[...], up_w[...])
    for to, at in enumerate(places):
        into = slice(to * rows, (to + 1) * rows)
        away[half + to * rows : half + (to + 1) * rows, :] = part[at * rows :][:rows].astype(BF16)
        up_home[into, :] = part[half + at * rows :][:rows]


def multiply_chunk(span, columns, weights, tok, rows, places):
    first, count = span
    n_tok, depth = tok.shape
    half = n_tok // 2
    weight = pl.BlockSpec((TILE, depth), lambda i: (first + i, 0))
    return pl.pallas_call(
        functools.partial(multiply_kernel, rows, places),
        grid=(count,),
        out_shape=[
            jax.ShapeDtypeStruct((n_tok, columns), BF16),
            jax.ShapeDtypeStruct((half, columns), F32),
            jax.ShapeDtypeStruct((half, columns), F32),
        ],
        in_specs=[pl.BlockSpec(tok.shape, lambda i: (0, 0)), weight, weight],
        out_specs=[
            pl.BlockSpec((n_tok, TILE), lambda i: (0, i)),
            pl.BlockSpec((half, TILE), lambda i: (0, i)),
            pl.BlockSpec((half, TILE), lambda i: (0, i)),
        ],
        compiler_params=pltpu.CompilerParams(
            dimension_semantics=("arbitrary",), vmem_limit_bytes=22 * 2**20
        ),
        cost_estimate=COST,
        name="multiply",
    )(tok, *weights)


def lower_kernel(rows, places, tok, low, old_away, old_gate, old_up, away, gate_home, up_home):
    rank = low.shape[0] // 2
    multiply_kernel(
        rows, places, tok, low.at[:rank, :], low.at[rank:, :], away, gate_home, up_home
    )


def multiply_lower(tok, low, part, rows, places):
    rank = low.shape[0] // 2
    last = part[0].shape[1] // rank - 1
    specs = [pl.BlockSpec((array.shape[0], rank), lambda i: (0, last)) for array in part]
    return pl.pallas_call(
        functools.partial(lower_kernel, rows, places),
        grid=(1,),
        out_shape=[jax.ShapeDtypeStruct(array.shape, array.dtype) for array in part],
        in_specs=[pl.BlockSpec(array.shape, lambda i: (0, 0)) for array in (tok, low)] + specs,
        out_specs=specs,
        input_output_aliases={2: 0, 3: 1, 4: 2},
        compiler_params=pltpu.CompilerParams(vmem_limit_bytes=12 * 2**20),
        cost_estimate=SMALL,
        name="multiply_lower",
    )(tok, low, *part)


def merge_kernel(low, gate_w, up_w, gate_b, gate_c, up_b, up_c, *refs):
    rank = gate_b.shape[0]
    for start in range(0, TILE, SUB):
        units = slice(start, start + SUB)
        for t, (weight, mine, other) in enumerate(
            ((gate_w, gate_b, gate_c), (up_w, up_b, up_c))
        ):
            delta = lax.dot_general(
                jnp.concatenate([mine[:, units], other[:, units]], axis=0),
                low[2 * t * rank : 2 * (t + 1) * rank, :],
                (((0,), (0,)), ((), ())),
                preferred_element_type=F32,
            )
            refs[t - 2][units, :] = (weight[units, :].astype(F32) + delta).astype(BF16)


def merge_span(span, weights, low, uppers, merged):
    first, count = span
    units, depth = weights[0].shape
    weight = pl.BlockSpec((TILE, depth), lambda i: (first + i, 0))
    upper = pl.BlockSpec((uppers[0].shape[0], TILE), lambda i: (0, first + i))
    operands = [low, *weights, *uppers, *merged]
    specs = [pl.BlockSpec(low.shape, lambda i: (0, 0)), weight, weight] + [upper] * 4
    specs += [pl.BlockSpec(memory_space=pl.ANY)] * len(merged)
    return pl.pallas_call(
        merge_kernel,
        grid=(count,),
        out_shape=[jax.ShapeDtypeStruct((units, depth), BF16)] * 2,
        in_specs=specs,
        out_specs=[weight] * 2,
        input_output_aliases={7: 0, 8: 1} if merged else {},
        compiler_params=pltpu.CompilerParams(
            dimension_semantics=("arbitrary",), vmem_limit_bytes=22 * 2**20
        ),
        cost_estimate=SMALL,
        name="merge",
    )(*operands)


class Sum:
    def __init__(self, away, gate, up, n_row):
        half = gate.shape[0]
        self.home = [gate, up]
        self.arrived = [swap(away, "row", n_row, 1)]
        self.places = [(0, 0, half), (0, half, half)]
        self.step = 0

    def came(self, t):
        array, start, size = self.places[t]
        return self.arrived[array][start : start + size].astype(F32)

    def finish(self):
        return [self.home[t] + self.came(t) for t in range(2)]


def exchange(items, orders, n_row):
    groups = {}
    for item in items:
        for t in range(2):
            home, came = item.home[t], item.came(t)
            half = home.shape[0] // 2
            groups.setdefault(orders[t][item.step], []).append(
                (item, t, (home[:half] + came[:half]).astype(BF16))
            )
            item.home[t] = home[half:] + came[half:]
    arrived, sent = [], []
    for number, (b, members) in enumerate(sorted(groups.items())):
        sent.append(jnp.concatenate([rows for _, _, rows in members], axis=0))
        arrived.append(swap(sent[-1], "row", n_row, 1 << b))
        start = 0
        for item, t, rows in members:
            item.places[t] = (number, start, rows.shape[0])
            start += rows.shape[0]
    for item in items:
        item.arrived = arrived
        item.step += 1
    return sent


def finish_kernel(gate_home, gate_came, up_home, up_came, sums, gate_b, gate_c, up_b, up_c, *refs):
    rank = 2 * gate_b.shape[0]
    high = sums[...].astype(BF16)
    low = (sums[...] - high.astype(F32)).astype(BF16)

    def total(home, came, mine, other, units, columns):
        upper = jnp.concatenate([mine[:, units], other[:, units]], axis=0)
        value = home[:, units] + came[:, units].astype(F32)
        for part in (high, low):
            value += jnp.dot(part[:, columns], upper, preferred_element_type=F32)
        return value

    for start in range(0, gate_home.shape[1], TILE):
        units = slice(start, start + TILE)
        gate = total(gate_home, gate_came, gate_b, gate_c, units, slice(0, rank))
        up = total(up_home, up_came, up_b, up_c, units, slice(rank, 2 * rank))
        refs[-1][:, units] = (jax.nn.silu(gate) * up).astype(BF16)


def finished(number, item, sums, uppers, units, hidden):
    rows, columns = item.home[0].shape
    home = pl.BlockSpec((rows, columns), lambda i: (0, 0))
    upper = pl.BlockSpec((uppers[0].shape[0], columns), lambda i: (0, number))
    operands, specs = [], []
    for t in range(2):
        array, start, _ = item.places[t]
        block = start // rows
        operands += [item.home[t], item.arrived[array]]
        specs += [home, pl.BlockSpec((rows, columns), lambda i, block=block: (block, 0))]
    operands += [sums, *uppers, *hidden]
    specs += [pl.BlockSpec(sums.shape, lambda i: (0, 0))] + [upper] * 4
    specs += [pl.BlockSpec(memory_space=pl.ANY)] * len(hidden)
    return pl.pallas_call(
        finish_kernel,
        grid=(1,),
        out_shape=[jax.ShapeDtypeStruct((rows, units), BF16)],
        in_specs=specs,
        out_specs=[pl.BlockSpec((rows, columns), lambda i: (0, number))],
        input_output_aliases={9: 0} if hidden else {},
        compiler_params=pltpu.CompilerParams(vmem_limit_bytes=14 * 2**20),
        name="finish",
    )(*operands)


def body(
    n_row, n_col, tokens, gate_weight, up_weight, gate_lower, up_lower, gate_upper, up_upper,
    outgoing, incoming,
):
    old, new = outgoing[0], incoming[0]
    row, col = lax.axis_index("row"), lax.axis_index("col")
    core = bit(row, 0)
    others = list(range(1, n_row.bit_length() - 1))
    orders = [others, others[1:] + others[:1]]
    stages = len(others)
    weights = [gate_weight.T, up_weight.T]
    units = weights[0].shape[0]
    rank = gate_upper.shape[1]
    tiles = pl.cdiv(pl.cdiv(units, 2 * rank) * 2 * rank + 2 * rank, TILE)
    per = pl.cdiv(tiles, CHUNKS)
    spans = [(first, min(per, tiles - first)) for first in range(0, tiles, per)]
    turns = list(range(len(spans)))
    turns[1:] = turns[:0:-1]
    used = pl.cdiv(units, TILE)

    state, sums = {"sent": []}, {}
    col_bits = list(range(n_col.bit_length() - 1))
    def slots(near, local):
        keep, other = jnp.where(near == 0, new, old), jnp.where(near == 0, old, new)
        return keep // local, [keep % local, other % local]

    upper_owner, upper_at = slots(bit(row, 0), gate_upper.shape[0])
    lower_owner, lower_at = slots(bit(col, 0), gate_lower.shape[0])

    def slot(stack, i):
        return lax.dynamic_index_in_dim(stack, i, 0, keepdims=False)

    offsets = [0]
    gathered = [swap(tokens, "col", n_col, 1 << col_bits[-1])]
    lowers = jnp.concatenate([jnp.swapaxes(a, 1, 2) for a in (gate_lower, up_lower)], axis=1)
    lower = Factor(
        "col", n_col, col, col_bits, *[slot(lowers, i) for i in lower_at], lower_owner
    )
    uppers = [
        Factor(
            "row", n_row, row, [0] + order, *[slot(stack, i) for i in upper_at], upper_owner
        )
        for stack, order in zip((gate_upper, up_upper), orders)
    ]

    def fence(*arrivals):
        items = list(sums.values())
        values = (
            state, [f.held for f in uppers + [lower]], [item.home for item in items],
            [item.arrived for item in arrivals],
        )
        values = lax.optimization_barrier(values)
        state.update(values[0])
        for factor, held in zip(uppers + [lower], values[1]):
            factor.held = held
        for item, home in zip(items, values[2]):
            item.home = home
        for item, arrived in zip(arrivals, values[3]):
            item.arrived = arrived

    def forward(*factors):
        state["sent"] = [state["sent"], [f.step() for f in factors if f.todo]]

    def running():
        return [f for f in uppers + [lower] if f.todo]

    def step():
        items = [sums[turn] for turn in turns if turn in sums]
        ready = [
            item for i, item in enumerate(items)
            if item.step < stages and (i == 0 or items[i - 1].step > item.step)
        ]
        if ready:
            state["sent"] = exchange(ready, orders, n_row)
        return ready

    for number, b in enumerate(reversed(col_bits)):
        fence()
        parts = [state.pop("parts", tokens)] + gathered
        offsets = offsets + [o ^ (1 << b) for o in offsets]
        if number + 1 < len(col_bits):
            state["parts"] = jnp.concatenate(parts, axis=0)
            gathered = [swap(state["parts"], "col", n_col, 1 << (b - 1))]
            forward(*uppers if number == 0 else (), lower)
    tok = state["tok"] = ordered_tokens(parts, offsets, n_row, row, col, orders[0])
    fence()
    forward(*uppers, lower)
    fence()

    rows = tok.shape[0] // n_row
    columns = per * TILE
    places = [block_order(orders[0]).index(k) for k in block_order(orders[1])]

    def low_factors():
        value = lower.joined()
        half = value.shape[0] // 2
        fresh, stale = value[:half], value[half:]
        return jnp.concatenate([fresh[:rank], -stale[:rank], fresh[rank:], -stale[rank:]], axis=0)

    flying = []
    for number, turn in enumerate(turns):
        part = multiply_chunk(spans[turn], columns, weights, state["tok"], rows, places)
        state["part"] = part
        fence(*running() if number < 2 else ())
        if number == 1 or len(turns) == 1:
            while lower.todo:
                forward(lower)
            state["low"] = low_factors()
            state["part"] = multiply_lower(state["tok"], state["low"], state["part"], rows, places)
        sums[turn] = Sum(*state.pop("part"), n_row)
        if number < 2:
            forward(*running())
        if number == 0:
            fence(sums[turn])
            flying = step()
        fence()
    fence(*flying, *[sums[turn] for turn in turns[1:2]])
    flying = step()
    fence()
    while running():
        fence(*uppers)
        forward(*uppers)
    fence(*uppers)

    def by_core(value, axis):
        parts = jnp.split(value, 4, axis=axis)
        turned = [parts[i] for i in (1, 0, 3, 2)]
        return jnp.where(
            core == 0, jnp.concatenate(parts, axis=axis), jnp.concatenate(turned, axis=axis)
        )

    state["uppers"] = [part for f in uppers for part in (f.held, f.arrived[0])]
    state["low"] = by_core(state["low"], 0)
    fence()
    cuts = [0, (used + 1) // 2, used, used]
    def finish(chosen, hidden):
        if chosen and "correction" not in state:
            ends = sums[turns[min(1, len(turns) - 1)]].finish()
            correction = jnp.concatenate([end[:, columns - 2 * rank :] for end in ends], axis=1)
            state["correction"] = by_core(correction, 1)
        for turn in chosen:
            hidden = finished(turn, sums[turn], state["correction"], state["uppers"], units, hidden)
        return hidden

    state["merged"] = []
    for first, last in zip(cuts, cuts[1:]):
        if last > first:
            state["merged"] = merge_span(
                (first, last - first), weights, state["low"], state["uppers"], state["merged"]
            )
        else:
            early = [t for t in turns[:-1] if all(sums[i].step == stages for i in turns[:-1])]
            state["hidden"] = finish(early, [])
        fence(*flying, *[sums[turn] for turn in turns[2:] if sums[turn].step == 0])
        flying = step()
        fence()
    while flying:
        flying = step()
    hidden = finish([turn for turn in turns if turn not in early], state["hidden"])
    merged = state["merged"]
    return merged[0].T, merged[1].T, hidden[0]


def solution(mesh):
    return jax.shard_map(
        functools.partial(body, mesh.shape["row"], mesh.shape["col"]),
        mesh=mesh,
        in_specs=(
            P("col", "row"),
            P("row", "col"),
            P("row", "col"),
            P("col", "row", None),
            P("col", "row", None),
            P("row", None, "col"),
            P("row", None, "col"),
            P(),
            P(),
        ),
        out_specs=(P("row", "col"), P("row", "col"), P("row", "col")),
        check_vma=False,
    )
```
